32 devices in a mesh: span: 2 (over y), tmpl: 2 (over x), stn: 8 (over z, core).
Axes of the slice: x: 2, y: 2, z: 4, core: 2. Of those that a mesh axis runs over, the one named last changes fastest.
Arguments:
- signal: bfloat16 [3072, 8192], P('stn', ('span', 'tmpl')), parts along dimension 1, may hold values from -110 to 110
- waveforms: bfloat16 [16, 4, 8, 300], P('tmpl'), may hold values from -40 to 40
- station_groups: int32 [16, 4], P('tmpl'), may hold values from 0 to 7, all different within a row; in each aligned block of 8 rows (0 to 7, 8 to 15, ...) at most 8 rows name the same one
- channel_offsets: int32 [16, 4, 8], P('tmpl'), may hold values from 0 to 383
- moveouts: int32 [16, 4, 8], P('tmpl'), may hold values from 0 to 639
Outputs:
- stack: float32 [16, 6144], P(('tmpl', 'stn'), 'span'), parts along dimension 1
The draws below stay inside these ranges and needn't reach their ends.
There are 2 independent parts, one for each index of `span`. The reference program is written for one: setup_inputs(seed, part) draws one part's arguments, and reference() takes and returns one part's arrays. A program takes and returns all parts, laid end to end along the dimension named above; an argument that names none is the same for every part. Nothing has to cross between parts.
Inputs may be any that keep to these rules, and one draw needn't show every extreme that they name: `station_groups`: A template's 4 station groups are distinct. Among the 8 templates of one index of tmpl, at most 8 touch any one station group, and in every draw some station group is touched by exactly 8 of them.
All inputs are finite; a program needn't handle non-finite values.
Results may differ from the reference program's by a relative error of at most 0.0003.
Values may be sent and summed in bfloat16 or wider, within the bound.
A program may use at most 64 MiB of HBM per device.

```python
import math
import jax
import jax.numpy as jnp
import numpy as np
from jax import lax

C = 3072
L = 300
SL = 8
TOUCH = 4
MV = 640
NT = 3072
TG = 8
K = 16
TCAP = 8
S = 4096
N_STN = 8


def draw_signal(key, part):
    key_scale, key_env, key_base = jax.random.split(key, 3)
    chan_scale = jnp.exp(jax.random.uniform(key_scale, (C, 1), minval=0.0, maxval=math.log(10.0)))
    envelope = jnp.exp(jax.random.uniform(key_env, (1, S // 128), minval=-0.7, maxval=0.7))
    envelope = jnp.repeat(envelope, 128, axis=1)
    base = jax.random.normal(key_base, (C, S))
    base = jnp.clip(base, -5.0, 5.0)
    return (base * chan_scale * envelope).astype(jnp.bfloat16)


def draw_waveforms(key, part):
    key_scale, key_base = jax.random.split(jax.random.fold_in(key, 7), 2)
    slot_scale = jnp.exp(jax.random.uniform(key_scale, (K, TOUCH, SL, 1), minval=0.0, maxval=math.log(10.0)))
    base = jnp.clip(jax.random.normal(key_base, (K, TOUCH, SL, L)), -4.0, 4.0)
    return (base * slot_scale).astype(jnp.bfloat16)


def place_ends(drawn, rng, low, high):
    shape = drawn.shape
    spot = [jax.random.randint(jax.random.fold_in(rng, axis), (), 0, shape[axis]) for axis in range(len(shape))]
    drawn = drawn.at[tuple(spot)].set(low)
    longest = shape.index(max(shape))
    spot[longest] = (spot[longest] + 1) % shape[longest]
    return drawn.at[tuple(spot)].set(high)


def shared_out(key, own, number, rows, amount, top, reach, skew):
    sequence = jax.random.permutation(key, amount)
    packed, usual = portions_of(amount, rows * top, reach, skew, True), portions_of(amount, rows * top, reach, skew, False)
    places = jnp.arange(amount)

    def named(sizes, offset_by):
        used = int((sizes > 0).sum())
        fixed = max(1, used // 4)
        moved = fixed + (places - fixed + offset_by * (used - fixed)) % max(1, amount - fixed)
        return jnp.zeros((amount,), jnp.int32).at[sequence[jnp.where(places < fixed, places, moved)]].set(jnp.asarray(sizes, jnp.int32))

    sizes = jnp.where(number % 4 == 0, named(packed, number // 4), named(usual, number - number // 4 - 1))
    mixed = jax.random.permutation(jax.random.fold_in(own, 3), amount)
    source_of, taker = mixed[0:amount // 2 * 2:2], mixed[1:amount // 2 * 2:2]
    slack = jnp.minimum(sizes[source_of] - 1, reach - sizes[taker]) // 2
    slack = jnp.where((source_of == sequence[0]) | (taker == sequence[0]) | (sizes[taker] == 0), 0, jnp.maximum(slack, 0))
    moved = jax.random.randint(jax.random.fold_in(own, 4), (amount // 2,), 0, 1 << 20) % (slack + 1)
    sizes = sizes.at[source_of].add(-moved).at[taker].add(moved)
    items = jnp.searchsorted(jnp.cumsum(sizes), jnp.arange(rows * top), side="right").astype(jnp.int32)
    listing = items.reshape(top, rows).T
    listing = listing[jax.random.permutation(jax.random.fold_in(own, 1), rows)]
    offset_by = jax.random.randint(jax.random.fold_in(own, 2), (rows, 1), 0, top)
    return jnp.take_along_axis(listing, (jnp.arange(top)[None, :] + offset_by) % top, axis=1)


def portions_of(amount, total, limit, slope, full):
    weights = [(1 << 20) // math.isqrt(rank ** slope) + 1 for rank in range(1, amount + 1)]
    largest = limit if full else min(limit, max(-(-total // amount), total * weights[0] // sum(weights)))
    least = 1 if total - largest >= amount - 1 else 0
    given, surplus = [largest] + [least] * (amount - 1), total - largest - least * (amount - 1)
    while surplus > 0:
        candidates = [i for i in range(1, amount) if given[i] < largest] or [i for i in range(1, amount) if given[i] < limit]
        mass, left = sum([weights[i] for i in candidates]), surplus
        for i in candidates:
            extra = min(limit - given[i], max(1, left * weights[i] // mass), surplus)
            given[i] = given[i] + extra
            surplus = surplus - extra
    return np.array(given)


def setup_inputs(seed: int = 0, part: int = 0) -> dict:
    seeds = jax.random.split(jax.random.key(seed), 6)
    own_keys = jax.random.split(jax.random.fold_in(seeds[5], part), 6)
    signal = draw_signal(jax.random.fold_in(jax.random.fold_in(seeds[5], part), 71), part)
    waveforms = draw_waveforms(jax.random.fold_in(seeds[5], 71), part)
    station_groups_keys = jax.random.split(jax.random.fold_in(seeds[2], 1), K // TG)
    station_groups_turns = jax.random.permutation(jax.random.fold_in(seeds[2], 3), K // TG)
    station_groups = jax.vmap(lambda own, number: shared_out(jax.random.fold_in(seeds[2], 2), own, number, TG, N_STN, TOUCH, TCAP, 2))(station_groups_keys, station_groups_turns).reshape((K, TOUCH))
    channel_offsets = place_ends(jax.random.randint(seeds[3], (K, TOUCH, SL), 0, C // N_STN), jax.random.fold_in(seeds[3], 1), 0, (C // N_STN) - 1).astype(jnp.int32)
    moveouts = place_ends(jax.random.randint(seeds[4], (K, TOUCH, SL), 0, MV), jax.random.fold_in(seeds[4], 1), 0, MV - 1).astype(jnp.int32)
    return {"signal": signal, "waveforms": waveforms, "station_groups": station_groups, "channel_offsets": channel_offsets, "moveouts": moveouts}


def reference(signal, waveforms, station_groups, channel_offsets, moveouts):
    data = signal.astype(jnp.float32)
    squares = data * data
    running = jnp.concatenate([jnp.zeros((C, 1), jnp.float32), jnp.cumsum(squares, axis=1)], axis=1)
    windows = running[:, L:] - running[:, :-L]
    rms_data = jnp.sqrt(windows / L + 1e-05)
    channel_of = (station_groups[:, :, None] * (C // N_STN) + channel_offsets).astype(jnp.int32)
    fft_len = NT + L

    def per_template(inputs):
        waves, chans, moves = inputs
        waves = waves.reshape(TOUCH * SL, L).astype(jnp.float32)
        chans = chans.reshape(TOUCH * SL)
        moves = moves.reshape(TOUCH * SL)

        def one_slot(channel, lag_shift):
            segment = lax.dynamic_slice(data, (channel, lag_shift), (1, NT + L - 1)).reshape(NT + L - 1)
            scale_row = lax.dynamic_slice(rms_data, (channel, lag_shift), (1, NT)).reshape(NT)
            return (segment, scale_row)
        segments, scales = jax.vmap(one_slot)(chans, moves)
        spectrum = jnp.fft.rfft(segments, n=fft_len) * jnp.conj(jnp.fft.rfft(waves, n=fft_len))
        correl = jnp.fft.irfft(spectrum, n=fft_len)[:, :NT]
        wave_rms = jnp.sqrt(lax.optimization_barrier(jnp.mean(waves * waves, axis=1)) + 1e-05)
        return lax.optimization_barrier(jnp.sum(correl / (L * wave_rms[:, None] * scales), axis=0))
    return lax.map(per_template, (waveforms, channel_of, moveouts))
```

```python
import functools

import jax
import jax.numpy as jnp
from jax import lax
from jax.experimental import pallas as pl
from jax.experimental.pallas import tpu as pltpu
from jax.sharding import PartitionSpec as P

NT = 3072
EPS = 1e-05
LANES = 128
ROWS = 16
MESH = pl.DeviceIdType.MESH
F32 = jnp.float32
BF16 = jnp.bfloat16


def iota(shape, axis):
    return lax.broadcasted_iota(jnp.int32, shape, axis)


def kernel(
    n_t, n_s, sg_ref, off_ref, mov_ref, wave_ref, sig_hbm, out_ref,
    pick, sig, asked, wanted, reply, landed, rows, toep, band, winv, wrev, stacks, parts,
    sig_sem, ask_send, ask_recv, row_send, row_recv, part_send, part_recv,
):
    me_t = lax.axis_index("tmpl")
    me_s = lax.axis_index("stn")
    n_k, touch = sg_ref.shape
    n_slot = off_ref.shape[2]
    length = wave_ref.shape[3]
    chans, span = sig.shape
    slots = n_k * n_slot
    span_blocks = span // LANES
    all_blocks = span_blocks * n_t
    n_circ = -(-length // LANES)
    n_band = n_circ + 1
    out_blocks = NT // LANES
    chunks = slots // ROWS
    per_chunk = ROWS // n_slot
    own = n_k // n_s

    load_sig = pltpu.make_async_copy(sig_hbm, sig, sig_sem)
    load_sig.start()

    barrier = pltpu.get_barrier_semaphore()
    for d in range(1, n_t):
        pl.semaphore_signal(
            barrier, inc=1, device_id={"tmpl": lax.rem(me_t + d, n_t)}, device_id_type=MESH
        )
    for d in range(1, n_s):
        pl.semaphore_signal(
            barrier, inc=1, device_id={"stn": lax.rem(me_s + d, n_s)}, device_id_type=MESH
        )

    sub = iota((n_slot, LANES), 0)
    for k in range(n_k):
        at = jnp.int32(0)
        for g in range(1, touch):
            at = jnp.where(sg_ref[k, g] == me_s, g, at)
        pick[k] = at
        tile = jnp.zeros((n_slot, LANES), jnp.int32)
        for s in range(n_slot):
            tile = jnp.where(sub == s, off_ref[k, at, s], tile)
        asked[k * n_slot : (k + 1) * n_slot, :] = tile

    pl.semaphore_wait(barrier, n_t - 1 + n_s - 1)

    def ask(d):
        return pltpu.make_async_remote_copy(
            src_ref=asked,
            dst_ref=wanted.at[d - 1],
            send_sem=ask_send.at[d - 1],
            recv_sem=ask_recv.at[d - 1],
            device_id={"tmpl": lax.rem(me_t + d, n_t)},
            device_id_type=MESH,
        )

    def send_rows(d, i):
        part = pl.ds(pl.multiple_of(i * ROWS, ROWS), ROWS)
        return pltpu.make_async_remote_copy(
            src_ref=reply.at[d - 1, part],
            dst_ref=landed.at[d - 1, part],
            send_sem=row_send.at[d - 1, i],
            recv_sem=row_recv.at[d - 1, i],
            device_id={"tmpl": lax.rem(me_t + n_t - d, n_t)},
            device_id_type=MESH,
        )

    for d in range(1, n_t):
        ask(d).start()

    piece = min(span, 512)

    def one_hot(ref):
        return (iota((slots, chans), 1) == ref[:, 0:1]).astype(F32).astype(BF16)

    def place(tile, source, first):
        count = tile.shape[0]
        for j in range(tile.shape[1] // LANES):
            start = first * all_blocks + source * span_blocks + j
            rows[pl.ds(start, count, stride=all_blocks), :] = tile[:, j * LANES : (j + 1) * LANES]

    load_sig.wait()
    mine = one_hot(asked)
    for c in range(span // piece):
        got = jnp.dot(mine, sig[:, c * piece : (c + 1) * piece], preferred_element_type=F32)
        for j in range(piece // LANES):
            start = me_t * span_blocks + c * (piece // LANES) + j
            rows[pl.ds(start, slots, stride=all_blocks), :] = got[:, j * LANES : (j + 1) * LANES]

    for d in range(1, n_t):
        ask(d).wait_recv()
        theirs = one_hot(wanted.at[d - 1])
        for c in range(span // piece):
            cut = slice(c * piece, (c + 1) * piece)
            reply[d - 1, :, cut] = jnp.dot(
                theirs, sig[:, cut], preferred_element_type=F32
            ).astype(BF16)
        for i in range(chunks):
            send_rows(d, i).start()

    waves = []
    for k in range(n_k):
        live = sg_ref[k, 0] == me_s
        for g in range(1, touch):
            live = jnp.logical_or(live, sg_ref[k, g] == me_s)
        wave = wave_ref[k, pick[k]].astype(F32)
        waves.append(jnp.where(live, wave, 0.0))
    waves = jnp.concatenate(waves, axis=0)
    power = jnp.sum(waves * waves, axis=1, keepdims=True) / length
    scale = lax.rsqrt(power + EPS) / length
    winv[...] = jnp.broadcast_to(scale, winv.shape)
    src = iota((length, n_circ * LANES), 0)
    dst = iota((length, n_circ * LANES), 1)
    turned = (src // LANES) * LANES + (LANES - src % LANES) % LANES
    flip = (dst == turned).astype(F32).astype(BF16)
    wrev[...] = jnp.dot(waves.astype(BF16), flip, preferred_element_type=F32)

    gap = iota((n_band * LANES, LANES), 0) - iota((n_band * LANES, LANES), 1)
    band[...] = jnp.logical_and(gap >= 0, gap < length).astype(F32).astype(BF16)

    lower = iota((LANES, LANES), 0) >= iota((LANES, LANES), 1)

    def build(k, carry):
        tile = wrev[pl.ds(pl.multiple_of(k * n_slot, n_slot), n_slot), :]
        for s in range(n_slot):
            before = jnp.zeros((LANES, LANES), F32)
            for j in range(n_band):
                if j < n_circ:
                    line = tile[s : s + 1, j * LANES : (j + 1) * LANES]
                    here = pltpu.roll(
                        jnp.broadcast_to(line, (LANES, LANES)), 0, 1, stride=1, stride_axis=0
                    )
                else:
                    here = jnp.zeros((LANES, LANES), F32)
                toep[k * n_slot + s, j * LANES : (j + 1) * LANES, :] = jnp.where(
                    lower, here, before
                ).astype(BF16)
                before = here
        return carry

    lax.fori_loop(0, n_k, build, 0)

    def send_part(k):
        return pltpu.make_async_remote_copy(
            src_ref=stacks.at[k],
            dst_ref=parts.at[me_s, lax.rem(k, own)],
            send_sem=part_send.at[k],
            recv_sem=part_recv.at[me_s, lax.rem(k, own)],
            device_id={"stn": k // own},
            device_id_type=MESH,
        )

    lane = iota((out_blocks, LANES), 1)

    def template(k, carry):
        at = pick[k]
        segs = []
        prods = []
        for s in range(n_slot):
            move = mov_ref[k, at, s]
            blocks = move // LANES
            rest = move - blocks * LANES
            turn = lax.rem(LANES - rest, LANES)
            base = (k * n_slot + s) * all_blocks + blocks
            turned = [
                pltpu.roll(rows[pl.ds(base + j, out_blocks), :], turn, 1) for j in range(n_band + 1)
            ]
            keep = lane < LANES - rest
            seg = jnp.concatenate(
                [jnp.where(keep, turned[j], turned[j + 1]) for j in range(n_band)], axis=1
            )
            segs.append(seg)
            prods.append(
                jnp.dot(seg.astype(BF16), toep[k * n_slot + s], preferred_element_type=F32)
            )
        seg = jnp.concatenate(segs, axis=0)
        square = seg * seg
        high = square.astype(BF16)
        low = (square - high.astype(F32)).astype(BF16)
        bands = band[...]
        energy = jnp.dot(high, bands, preferred_element_type=F32)
        energy = energy + jnp.dot(low, bands, preferred_element_type=F32)
        inverse = lax.rsqrt(energy / length + EPS)
        scales = winv[pl.ds(pl.multiple_of(k * n_slot, n_slot), n_slot), :]
        total = jnp.zeros((out_blocks, LANES), F32)
        for s in range(n_slot):
            part = inverse[s * out_blocks : (s + 1) * out_blocks]
            total = total + prods[s] * (part * scales[s : s + 1, :])
        stacks[k] = total

        @pl.when(k // own != me_s)
        def _():
            send_part(k).start()

        return carry

    def chunk(i, carry):
        for d in range(1, n_t):
            send_rows(d, i).wait_recv()
            tile = landed[d - 1, pl.ds(pl.multiple_of(i * ROWS, ROWS), ROWS), :].astype(F32)
            place(tile, lax.rem(me_t + d, n_t), i * ROWS)
        return lax.fori_loop(i * per_chunk, (i + 1) * per_chunk, template, carry)

    lax.fori_loop(0, chunks, chunk, 0)

    for d in range(1, n_t):
        ask(d).wait_send()
        for i in range(chunks):
            send_rows(d, i).wait_send()

    for r in range(own):
        out_ref[r] = stacks[me_s * own + r]
    for d in range(1, n_s):
        other = lax.rem(me_s + d, n_s)
        for r in range(own):
            pltpu.make_async_remote_copy(
                src_ref=stacks.at[0],
                dst_ref=parts.at[other, r],
                send_sem=part_send.at[0],
                recv_sem=part_recv.at[other, r],
                device_id={"stn": other},
                device_id_type=MESH,
            ).wait_recv()
            out_ref[r] = out_ref[r] + parts[other, r]
    for d in range(1, n_s):
        other = lax.rem(me_s + d, n_s)
        for r in range(own):
            send_part(other * own + r).wait_send()


def shards(signal, waveforms, station_groups, channel_offsets, moveouts):
    n_t = lax.axis_size("tmpl")
    n_s = lax.axis_size("stn")
    n_k, touch, n_slot, length = waveforms.shape
    chans, span = signal.shape
    slots = n_k * n_slot
    out_blocks = NT // LANES
    n_circ = -(-length // LANES)
    chunks = slots // ROWS
    own = n_k // n_s
    smem = pl.BlockSpec(memory_space=pltpu.SMEM)
    vmem = pl.BlockSpec(memory_space=pltpu.VMEM)
    dma = pltpu.SemaphoreType.DMA
    stack = pl.pallas_call(
        functools.partial(kernel, n_t, n_s),
        out_shape=jax.ShapeDtypeStruct((own, out_blocks, LANES), F32),
        in_specs=[smem, smem, smem, vmem, pl.BlockSpec(memory_space=pl.ANY)],
        out_specs=vmem,
        scratch_shapes=[
            pltpu.SMEM((n_k,), jnp.int32),
            pltpu.VMEM((chans, span), BF16),
            pltpu.VMEM((slots, LANES), jnp.int32),
            pltpu.VMEM((n_t - 1, slots, LANES), jnp.int32),
            pltpu.VMEM((n_t - 1, slots, span), BF16),
            pltpu.VMEM((n_t - 1, slots, span), BF16),
            pltpu.VMEM((slots * n_t * span // LANES, LANES), F32),
            pltpu.VMEM((slots, (n_circ + 1) * LANES, LANES), BF16),
            pltpu.VMEM(((n_circ + 1) * LANES, LANES), BF16),
            pltpu.VMEM((slots, LANES), F32),
            pltpu.VMEM((slots, n_circ * LANES), F32),
            pltpu.VMEM((n_k, out_blocks, LANES), F32),
            pltpu.VMEM((n_s, own, out_blocks, LANES), F32),
            dma,
            dma((n_t - 1,)),
            dma((n_t - 1,)),
            dma((n_t - 1, chunks)),
            dma((n_t - 1, chunks)),
            dma((n_k,)),
            dma((n_s, own)),
        ],
        compiler_params=pltpu.CompilerParams(
            collective_id=0, has_side_effects=True, vmem_limit_bytes=50 * 1024 * 1024
        ),
    )(station_groups, channel_offsets, moveouts, waveforms, signal)
    return stack.reshape(own, NT)


def solution(mesh):
    in_specs = (
        P("stn", ("span", "tmpl")),
        P("tmpl", None, None, None),
        P("tmpl", None),
        P("tmpl", None, None),
        P("tmpl", None, None),
    )
    out_specs = P(("tmpl", "stn"), "span")
    return jax.shard_map(shards, mesh=mesh, in_specs=in_specs, out_specs=out_specs, check_vma=False)
```

```python
import functools

import jax
import jax.numpy as jnp
from jax import lax
from jax.experimental import pallas as pl
from jax.experimental.pallas import tpu as pltpu
from jax.sharding import PartitionSpec as P

NT = 3072
EPS = 1e-05
LANES = 128
ROWS = 16
MESH = pl.DeviceIdType.MESH
F32 = jnp.float32
BF16 = jnp.bfloat16


def iota(shape, axis):
    return lax.broadcasted_iota(jnp.int32, shape, axis)


def kernel(
    n_t, n_s, sg_hbm, off_hbm, mov_hbm, wave_hbm, sig_hbm, out_ref,
    sg_ref, off_ref, mov_ref, wave_ref, pick, sig, asked, wanted, reply, landed, rows, toep, band, winv, wrev, stacks, parts,
    load_sem, ask_send, ask_recv, row_send, row_recv, part_send, part_recv,
):
    me_t = lax.axis_index("tmpl")
    me_s = lax.axis_index("stn")
    touch, n_k = sg_ref.shape
    n_slot = off_ref.shape[2]
    length = wave_ref.shape[3]
    chans, span = sig.shape
    slots = n_k * n_slot
    span_blocks = span // LANES
    all_blocks = span_blocks * n_t
    n_circ = -(-length // LANES)
    n_band = n_circ + 1
    out_blocks = NT // LANES
    chunks = slots // ROWS
    per_chunk = ROWS // n_slot
    own = n_k // n_s

    barrier = pltpu.get_barrier_semaphore()
    for d in range(1, n_t):
        pl.semaphore_signal(
            barrier, inc=1, device_id={"tmpl": lax.rem(me_t + d, n_t)}, device_id_type=MESH
        )
    for d in range(1, n_s):
        pl.semaphore_signal(
            barrier, inc=1, device_id={"stn": lax.rem(me_s + d, n_s)}, device_id_type=MESH
        )

    operands = (
        (sg_hbm, sg_ref), (off_hbm, off_ref), (sig_hbm, sig), (wave_hbm, wave_ref), (mov_hbm, mov_ref)
    )
    loads = [
        pltpu.make_async_copy(a, b, load_sem.at[i]) for i, (a, b) in enumerate(operands)
    ]
    for load in loads:
        load.start()

    gap = iota((n_band * LANES, LANES), 0) - iota((n_band * LANES, LANES), 1)
    band[...] = jnp.logical_and(gap >= 0, gap < length).astype(F32).astype(BF16)
    turn = jnp.bitwise_and(iota((LANES, LANES), 0) + iota((LANES, LANES), 1), LANES - 1)
    flip = (turn == 0).astype(F32).astype(BF16)

    loads[0].wait()
    loads[1].wait()

    sub = iota((n_slot, LANES), 0)
    for k in range(n_k):
        at = jnp.int32(0)
        for g in range(1, touch):
            at = jnp.where(sg_ref[g, k] == me_s, g, at)
        pick[k] = at
        tile = jnp.zeros((n_slot, LANES), jnp.int32)
        for s in range(n_slot):
            tile = jnp.where(sub == s, off_ref[k, at, s], tile)
        asked[k * n_slot : (k + 1) * n_slot, :] = tile

    pl.semaphore_wait(barrier, n_t - 1 + n_s - 1)

    def ask(d):
        return pltpu.make_async_remote_copy(
            src_ref=asked,
            dst_ref=wanted.at[d - 1],
            send_sem=ask_send.at[d - 1],
            recv_sem=ask_recv.at[d - 1],
            device_id={"tmpl": lax.rem(me_t + d, n_t)},
            device_id_type=MESH,
        )

    def send_rows(d, i):
        part = pl.ds(pl.multiple_of(i * ROWS, ROWS), ROWS)
        return pltpu.make_async_remote_copy(
            src_ref=reply.at[d - 1, part],
            dst_ref=landed.at[d - 1, part],
            send_sem=row_send.at[d - 1, i],
            recv_sem=row_recv.at[d - 1, i],
            device_id={"tmpl": lax.rem(me_t + n_t - d, n_t)},
            device_id_type=MESH,
        )

    for d in range(1, n_t):
        ask(d).start()

    piece = min(span, 512)

    def one_hot(ref):
        return (iota((slots, chans), 1) == ref[:, 0:1]).astype(F32).astype(BF16)

    def place(tile, source, first):
        count = tile.shape[0]
        for j in range(tile.shape[1] // LANES):
            start = first * all_blocks + source * span_blocks + j
            rows[pl.ds(start, count, stride=all_blocks), :] = tile[:, j * LANES : (j + 1) * LANES]

    loads[2].wait()
    mine = one_hot(asked)
    for c in range(span // piece):
        got = jnp.dot(mine, sig[:, c * piece : (c + 1) * piece], preferred_element_type=F32)
        for j in range(piece // LANES):
            start = me_t * span_blocks + c * (piece // LANES) + j
            rows[pl.ds(start, slots, stride=all_blocks), :] = got[:, j * LANES : (j + 1) * LANES]

    loads[3].wait()
    waves = []
    for k in range(n_k):
        live = sg_ref[0, k] == me_s
        for g in range(1, touch):
            live = jnp.logical_or(live, sg_ref[g, k] == me_s)
        wave = wave_ref[k, pick[k]].astype(F32)
        waves.append(jnp.where(live, wave, 0.0))
    waves = jnp.concatenate(waves, axis=0)
    power = jnp.sum(waves * waves, axis=1, keepdims=True) / length
    scale = lax.rsqrt(power + EPS) / length
    winv[...] = jnp.broadcast_to(scale, winv.shape)
    for j in range(n_circ):
        count = min(LANES, length - j * LANES)
        wrev[:, j * LANES : (j + 1) * LANES] = jnp.dot(
            waves[:, j * LANES : j * LANES + count].astype(BF16),
            flip[:count],
            preferred_element_type=F32,
        )

    for d in range(1, n_t):
        ask(d).wait_recv()
        theirs = one_hot(wanted.at[d - 1])
        for c in range(span // piece):
            cut = slice(c * piece, (c + 1) * piece)
            reply[d - 1, :, cut] = jnp.dot(
                theirs, sig[:, cut], preferred_element_type=F32
            ).astype(BF16)
        for i in range(chunks):
            send_rows(d, i).start()

    lower = (iota((LANES, LANES), 0) >= iota((LANES, LANES), 1)).astype(F32).astype(BF16) > 0

    def circle(line):
        first = pltpu.roll(jnp.broadcast_to(line, (ROWS, LANES)), 0, 1, stride=1, stride_axis=0)
        first = first.astype(BF16)
        return jnp.concatenate(
            [first] + [pltpu.roll(first, r, 1) for r in range(ROWS, LANES, ROWS)], axis=0
        )

    def build(k, carry):
        tile = wrev[pl.ds(pl.multiple_of(k * n_slot, n_slot), n_slot), :]
        zero = jnp.zeros((LANES, LANES), BF16)
        for s in range(n_slot):
            before = zero
            for j in range(n_band):
                here = zero
                if j < n_circ:
                    here = circle(tile[s : s + 1, j * LANES : (j + 1) * LANES])
                toep[k * n_slot + s, j * LANES : (j + 1) * LANES, :] = jnp.where(
                    lower, here, before
                )
                before = here
        return carry

    lax.fori_loop(0, n_k, build, 0)

    def send_part(k):
        return pltpu.make_async_remote_copy(
            src_ref=stacks.at[k],
            dst_ref=parts.at[me_s, lax.rem(k, own)],
            send_sem=part_send.at[k],
            recv_sem=part_recv.at[me_s, lax.rem(k, own)],
            device_id={"stn": k // own},
            device_id_type=MESH,
        )

    lane = iota((out_blocks, LANES), 1)
    loads[4].wait()

    def template(k, carry):
        at = pick[k]
        segs = []
        prods = []
        for s in range(n_slot):
            move = mov_ref[k, at, s]
            blocks = move // LANES
            rest = move - blocks * LANES
            turn = lax.rem(LANES - rest, LANES)
            base = (k * n_slot + s) * all_blocks + blocks
            turned = [
                pltpu.roll(rows[pl.ds(base + j, out_blocks), :], turn, 1) for j in range(n_band + 1)
            ]
            keep = lane < LANES - rest
            seg = jnp.concatenate(
                [jnp.where(keep, turned[j], turned[j + 1]) for j in range(n_band)], axis=1
            )
            segs.append(seg)
            prods.append(
                jnp.dot(seg.astype(BF16), toep[k * n_slot + s], preferred_element_type=F32)
            )
        seg = jnp.concatenate(segs, axis=0)
        square = seg * seg
        high = square.astype(BF16)
        low = (square - high.astype(F32)).astype(BF16)
        bands = band[...]
        energy = jnp.dot(high, bands, preferred_element_type=F32)
        energy = energy + jnp.dot(low, bands, preferred_element_type=F32)
        inverse = lax.rsqrt(energy / length + EPS)
        scales = winv[pl.ds(pl.multiple_of(k * n_slot, n_slot), n_slot), :]
        total = jnp.zeros((out_blocks, LANES), F32)
        for s in range(n_slot):
            part = inverse[s * out_blocks : (s + 1) * out_blocks]
            total = total + prods[s] * (part * scales[s : s + 1, :])
        stacks[k] = total

        @pl.when(k // own != me_s)
        def _():
            send_part(k).start()

        return carry

    def chunk(i, carry):
        for d in range(1, n_t):
            send_rows(d, i).wait_recv()
            tile = landed[d - 1, pl.ds(pl.multiple_of(i * ROWS, ROWS), ROWS), :].astype(F32)
            place(tile, lax.rem(me_t + d, n_t), i * ROWS)
        return lax.fori_loop(i * per_chunk, (i + 1) * per_chunk, template, carry)

    lax.fori_loop(0, chunks, chunk, 0)

    for d in range(1, n_t):
        ask(d).wait_send()
        for i in range(chunks):
            send_rows(d, i).wait_send()

    for r in range(own):
        out_ref[r] = stacks[me_s * own + r]
    for d in range(1, n_s):
        other = lax.rem(me_s + d, n_s)
        for r in range(own):
            pltpu.make_async_remote_copy(
                src_ref=stacks.at[0],
                dst_ref=parts.at[other, r],
                send_sem=part_send.at[0],
                recv_sem=part_recv.at[other, r],
                device_id={"stn": other},
                device_id_type=MESH,
            ).wait_recv()
            out_ref[r] = out_ref[r] + parts[other, r]
    for d in range(1, n_s):
        other = lax.rem(me_s + d, n_s)
        for r in range(own):
            send_part(other * own + r).wait_send()


def shards(signal, waveforms, station_groups, channel_offsets, moveouts):
    n_t = lax.axis_size("tmpl")
    n_s = lax.axis_size("stn")
    n_k, touch, n_slot, length = waveforms.shape
    chans, span = signal.shape
    slots = n_k * n_slot
    out_blocks = NT // LANES
    n_circ = -(-length // LANES)
    chunks = slots // ROWS
    own = n_k // n_s
    dma = pltpu.SemaphoreType.DMA
    stack = pl.pallas_call(
        functools.partial(kernel, n_t, n_s),
        out_shape=jax.ShapeDtypeStruct((own, out_blocks, LANES), F32),
        in_specs=[pl.BlockSpec(memory_space=pl.ANY)] * 5,
        out_specs=pl.BlockSpec(memory_space=pltpu.VMEM),
        scratch_shapes=[
            pltpu.SMEM((touch, n_k), jnp.int32),
            pltpu.SMEM((n_k, touch, n_slot), jnp.int32),
            pltpu.SMEM((n_k, touch, n_slot), jnp.int32),
            pltpu.VMEM((n_k, touch, n_slot, length), BF16),
            pltpu.SMEM((n_k,), jnp.int32),
            pltpu.VMEM((chans, span), BF16),
            pltpu.VMEM((slots, LANES), jnp.int32),
            pltpu.VMEM((n_t - 1, slots, LANES), jnp.int32),
            pltpu.VMEM((n_t - 1, slots, span), BF16),
            pltpu.VMEM((n_t - 1, slots, span), BF16),
            pltpu.VMEM((slots * n_t * span // LANES, LANES), F32),
            pltpu.VMEM((slots, (n_circ + 1) * LANES, LANES), BF16),
            pltpu.VMEM(((n_circ + 1) * LANES, LANES), BF16),
            pltpu.VMEM((slots, LANES), F32),
            pltpu.VMEM((slots, n_circ * LANES), F32),
            pltpu.VMEM((n_k, out_blocks, LANES), F32),
            pltpu.VMEM((n_s, own, out_blocks, LANES), F32),
            dma((5,)),
            dma((n_t - 1,)),
            dma((n_t - 1,)),
            dma((n_t - 1, chunks)),
            dma((n_t - 1, chunks)),
            dma((n_k,)),
            dma((n_s, own)),
        ],
        compiler_params=pltpu.CompilerParams(
            collective_id=0, has_side_effects=True, vmem_limit_bytes=63 * 1024 * 1024
        ),
    )(station_groups.T, channel_offsets, moveouts, waveforms, signal)
    return stack.reshape(own, NT)


def solution(mesh):
    in_specs = (
        P("stn", ("span", "tmpl")),
        P("tmpl", None, None, None),
        P("tmpl", None),
        P("tmpl", None, None),
        P("tmpl", None, None),
    )
    out_specs = P(("tmpl", "stn"), "span")
    return jax.shard_map(shards, mesh=mesh, in_specs=in_specs, out_specs=out_specs, check_vma=False)
```

```python
import functools

import jax
import jax.numpy as jnp
from jax import lax
from jax.experimental import pallas as pl
from jax.experimental.pallas import tpu as pltpu
from jax.sharding import PartitionSpec as P

NT = 3072
EPS = 1e-05
LANES = 128
ROWS = 16
MESH = pl.DeviceIdType.MESH
F32 = jnp.float32
BF16 = jnp.bfloat16


def iota(shape, axis):
    return lax.broadcasted_iota(jnp.int32, shape, axis)


def kernel(
    n_t, n_s, sg_hbm, off_hbm, mov_hbm, wave_hbm, sig_hbm, out_ref,
    sg_ref, off_ref, mov_ref, wave_ref, pick, sig, asked, wanted, reply, landed, rows, toep, band, winv, wrev, stacks, parts,
    load_sem, ask_send, ask_recv, row_send, row_recv, part_send, part_recv,
):
    me_t = lax.axis_index("tmpl")
    me_s = lax.axis_index("stn")
    touch, n_k = sg_ref.shape
    n_slot = off_ref.shape[2]
    length = wave_ref.shape[3]
    chans, span = sig.shape
    slots = n_k * n_slot
    span_blocks = span // LANES
    all_blocks = span_blocks * n_t
    n_circ = -(-length // LANES)
    n_band = n_circ + 1
    out_blocks = NT // LANES
    chunks = slots // ROWS
    per_chunk = ROWS // n_slot
    own = n_k // n_s

    barrier = pltpu.get_barrier_semaphore()
    for d in range(1, n_t):
        pl.semaphore_signal(
            barrier, inc=1, device_id={"tmpl": lax.rem(me_t + d, n_t)}, device_id_type=MESH
        )
    for d in range(1, n_s):
        pl.semaphore_signal(
            barrier, inc=1, device_id={"stn": lax.rem(me_s + d, n_s)}, device_id_type=MESH
        )

    operands = (
        (sg_hbm, sg_ref), (off_hbm, off_ref), (sig_hbm, sig), (wave_hbm, wave_ref), (mov_hbm, mov_ref)
    )
    loads = [
        pltpu.make_async_copy(a, b, load_sem.at[i]) for i, (a, b) in enumerate(operands)
    ]
    for load in loads:
        load.start()

    gap = iota((n_band * LANES, LANES), 0) - iota((n_band * LANES, LANES), 1)
    band[...] = jnp.logical_and(gap >= 0, gap < length).astype(F32).astype(BF16)
    turn = jnp.bitwise_and(iota((LANES, LANES), 0) + iota((LANES, LANES), 1), LANES - 1)
    flip = (turn == 0).astype(F32).astype(BF16)

    loads[0].wait()
    loads[1].wait()

    lane = iota((n_slot, LANES), 1)
    sub = iota((n_slot, LANES), 0)
    tile = jnp.zeros((n_slot, LANES), jnp.int32)
    for k in range(n_k):
        at = jnp.int32(0)
        for g in range(1, touch):
            at = jnp.where(sg_ref[g, k] == me_s, g, at)
        pick[k] = at
        column = jnp.zeros((n_slot, LANES), jnp.int32)
        for s in range(n_slot):
            column = jnp.where(sub == s, off_ref[k, at, s], column)
        tile = jnp.where(lane == k, column, tile)
    asked[...] = tile

    pl.semaphore_wait(barrier, n_t - 1 + n_s - 1)

    def ask(d):
        return pltpu.make_async_remote_copy(
            src_ref=asked,
            dst_ref=wanted.at[d - 1],
            send_sem=ask_send.at[d - 1],
            recv_sem=ask_recv.at[d - 1],
            device_id={"tmpl": lax.rem(me_t + d, n_t)},
            device_id_type=MESH,
        )

    def send_rows(d, i):
        part = pl.ds(pl.multiple_of(i * ROWS, ROWS), ROWS)
        return pltpu.make_async_remote_copy(
            src_ref=reply.at[d - 1, part],
            dst_ref=landed.at[d - 1, part],
            send_sem=row_send.at[d - 1, i],
            recv_sem=row_recv.at[d - 1, i],
            device_id={"tmpl": lax.rem(me_t + n_t - d, n_t)},
            device_id_type=MESH,
        )

    for d in range(1, n_t):
        ask(d).start()

    piece = min(span, 512)

    def one_hot(tile):
        number = iota((n_slot, chans), 1)
        picked = [
            (number == jnp.broadcast_to(tile[:, k : k + 1], (n_slot, chans))).astype(F32)
            for k in range(n_k)
        ]
        return jnp.concatenate(picked, axis=0).astype(BF16)

    def order(i):
        return lax.rem(me_s * own // per_chunk + 1 + i, chunks)

    def place(tile, source, first):
        count = tile.shape[0]
        for j in range(tile.shape[1] // LANES):
            start = first * all_blocks + source * span_blocks + j
            rows[pl.ds(start, count, stride=all_blocks), :] = tile[:, j * LANES : (j + 1) * LANES]

    loads[2].wait()
    mine = one_hot(tile)
    for c in range(span // piece):
        got = jnp.dot(mine, sig[:, c * piece : (c + 1) * piece], preferred_element_type=F32)
        for j in range(piece // LANES):
            start = me_t * span_blocks + c * (piece // LANES) + j
            rows[pl.ds(start, slots, stride=all_blocks), :] = got[:, j * LANES : (j + 1) * LANES]

    for d in range(1, n_t):
        ask(d).wait_recv()
        theirs = one_hot(wanted[d - 1])
        for c in range(span // piece):
            cut = slice(c * piece, (c + 1) * piece)
            reply[d - 1, :, cut] = jnp.dot(
                theirs, sig[:, cut], preferred_element_type=F32
            ).astype(BF16)
        for i in range(chunks):
            send_rows(d, order(i)).start()

    loads[3].wait()
    waves = []
    for k in range(n_k):
        live = sg_ref[0, k] == me_s
        for g in range(1, touch):
            live = jnp.logical_or(live, sg_ref[g, k] == me_s)
        wave = wave_ref[k, pick[k]].astype(F32)
        waves.append(jnp.where(live, wave, 0.0))
    waves = jnp.concatenate(waves, axis=0)
    power = jnp.sum(waves * waves, axis=1, keepdims=True) / length
    scale = lax.rsqrt(power + EPS) / length
    winv[...] = jnp.broadcast_to(scale, winv.shape)
    for j in range(n_circ):
        count = min(LANES, length - j * LANES)
        wrev[:, j * LANES : (j + 1) * LANES] = jnp.dot(
            waves[:, j * LANES : j * LANES + count].astype(BF16),
            flip[:count],
            preferred_element_type=F32,
        )

    lower = (iota((LANES, LANES), 0) >= iota((LANES, LANES), 1)).astype(F32).astype(BF16) > 0

    def circle(line):
        first = pltpu.roll(jnp.broadcast_to(line, (ROWS, LANES)), 0, 1, stride=1, stride_axis=0)
        first = first.astype(BF16)
        return jnp.concatenate(
            [first] + [pltpu.roll(first, r, 1) for r in range(ROWS, LANES, ROWS)], axis=0
        )

    def build(k, carry):
        tile = wrev[pl.ds(pl.multiple_of(k * n_slot, n_slot), n_slot), :]
        zero = jnp.zeros((LANES, LANES), BF16)
        for s in range(n_slot):
            before = zero
            for j in range(n_band):
                here = zero
                if j < n_circ:
                    here = circle(tile[s : s + 1, j * LANES : (j + 1) * LANES])
                toep[k * n_slot + s, j * LANES : (j + 1) * LANES, :] = jnp.where(
                    lower, here, before
                )
                before = here
        return carry

    lax.fori_loop(0, n_k, build, 0)

    def send_part(k):
        return pltpu.make_async_remote_copy(
            src_ref=stacks.at[k],
            dst_ref=parts.at[me_s, lax.rem(k, own)],
            send_sem=part_send.at[k],
            recv_sem=part_recv.at[me_s, lax.rem(k, own)],
            device_id={"stn": k // own},
            device_id_type=MESH,
        )

    spot = iota((out_blocks, LANES), 1)
    loads[4].wait()

    def template(k):
        at = pick[k]
        segs = []
        prods = []
        for s in range(n_slot):
            move = mov_ref[k, at, s]
            blocks = move // LANES
            rest = move - blocks * LANES
            turn = lax.rem(LANES - rest, LANES)
            base = (k * n_slot + s) * all_blocks + blocks
            turned = [
                pltpu.roll(rows[pl.ds(base + j, out_blocks), :], turn, 1) for j in range(n_band + 1)
            ]
            keep = spot < LANES - rest
            seg = jnp.concatenate(
                [jnp.where(keep, turned[j], turned[j + 1]) for j in range(n_band)], axis=1
            )
            segs.append(seg)
            prods.append(
                jnp.dot(seg.astype(BF16), toep[k * n_slot + s], preferred_element_type=F32)
            )
        seg = jnp.concatenate(segs, axis=0)
        square = seg * seg
        high = square.astype(BF16)
        low = (square - high.astype(F32)).astype(BF16)
        bands = band[...]
        energy = jnp.dot(high, bands, preferred_element_type=F32)
        energy = energy + jnp.dot(low, bands, preferred_element_type=F32)
        inverse = lax.rsqrt(energy / length + EPS)
        scales = winv[pl.ds(pl.multiple_of(k * n_slot, n_slot), n_slot), :]
        total = jnp.zeros((out_blocks, LANES), F32)
        for s in range(n_slot):
            part = inverse[s * out_blocks : (s + 1) * out_blocks]
            total = total + prods[s] * (part * scales[s : s + 1, :])
        return total

    def chunk(step, carry):
        i = order(step)
        for d in range(1, n_t):
            send_rows(d, i).wait_recv()
            tile = landed[d - 1, pl.ds(pl.multiple_of(i * ROWS, ROWS), ROWS), :].astype(F32)
            place(tile, lax.rem(me_t + d, n_t), i * ROWS)
        names = [
            i * per_chunk + lax.rem(me_s * own + 1 + q, per_chunk) for q in range(per_chunk)
        ]
        totals = [template(k) for k in names]
        for k, total in zip(names, totals):
            stacks[k] = total
        for k in names:

            @pl.when(k // own != me_s)
            def _(k=k):
                send_part(k).start()

        return carry

    lax.fori_loop(0, chunks, chunk, 0)

    for d in range(1, n_t):
        ask(d).wait_send()
        for i in range(chunks):
            send_rows(d, i).wait_send()

    for r in range(own):
        out_ref[r] = stacks[me_s * own + r]
    for d in range(1, n_s):
        other = lax.rem(me_s + d, n_s)
        for r in range(own):
            pltpu.make_async_remote_copy(
                src_ref=stacks.at[0],
                dst_ref=parts.at[other, r],
                send_sem=part_send.at[0],
                recv_sem=part_recv.at[other, r],
                device_id={"stn": other},
                device_id_type=MESH,
            ).wait_recv()
            out_ref[r] = out_ref[r] + parts[other, r]
    for d in range(1, n_s):
        other = lax.rem(me_s + d, n_s)
        for r in range(own):
            send_part(other * own + r).wait_send()


def shards(signal, waveforms, station_groups, channel_offsets, moveouts):
    n_t = lax.axis_size("tmpl")
    n_s = lax.axis_size("stn")
    n_k, touch, n_slot, length = waveforms.shape
    chans, span = signal.shape
    slots = n_k * n_slot
    out_blocks = NT // LANES
    n_circ = -(-length // LANES)
    chunks = slots // ROWS
    own = n_k // n_s
    dma = pltpu.SemaphoreType.DMA
    stack = pl.pallas_call(
        functools.partial(kernel, n_t, n_s),
        out_shape=jax.ShapeDtypeStruct((own, out_blocks, LANES), F32),
        in_specs=[pl.BlockSpec(memory_space=pl.ANY)] * 5,
        out_specs=pl.BlockSpec(memory_space=pltpu.VMEM),
        scratch_shapes=[
            pltpu.SMEM((touch, n_k), jnp.int32),
            pltpu.SMEM((n_k, touch, n_slot), jnp.int32),
            pltpu.SMEM((n_k, touch, n_slot), jnp.int32),
            pltpu.VMEM((n_k, touch, n_slot, length), BF16),
            pltpu.SMEM((n_k,), jnp.int32),
            pltpu.VMEM((chans, span), BF16),
            pltpu.VMEM((n_slot, LANES), jnp.int32),
            pltpu.VMEM((n_t - 1, n_slot, LANES), jnp.int32),
            pltpu.VMEM((n_t - 1, slots, span), BF16),
            pltpu.VMEM((n_t - 1, slots, span), BF16),
            pltpu.VMEM((slots * n_t * span // LANES, LANES), F32),
            pltpu.VMEM((slots, (n_circ + 1) * LANES, LANES), BF16),
            pltpu.VMEM(((n_circ + 1) * LANES, LANES), BF16),
            pltpu.VMEM((slots, LANES), F32),
            pltpu.VMEM((slots, n_circ * LANES), F32),
            pltpu.VMEM((n_k, out_blocks, LANES), F32),
            pltpu.VMEM((n_s, own, out_blocks, LANES), F32),
            dma((5,)),
            dma((n_t - 1,)),
            dma((n_t - 1,)),
            dma((n_t - 1, chunks)),
            dma((n_t - 1, chunks)),
            dma((n_k,)),
            dma((n_s, own)),
        ],
        compiler_params=pltpu.CompilerParams(
            collective_id=0, has_side_effects=True, vmem_limit_bytes=63 * 1024 * 1024
        ),
    )(station_groups.T, channel_offsets, moveouts, waveforms, signal)
    return stack.reshape(own, NT)


def solution(mesh):
    in_specs = (
        P("stn", ("span", "tmpl")),
        P("tmpl", None, None, None),
        P("tmpl", None),
        P("tmpl", None, None),
        P("tmpl", None, None),
    )
    out_specs = P(("tmpl", "stn"), "span")
    return jax.shard_map(shards, mesh=mesh, in_specs=in_specs, out_specs=out_specs, check_vma=False)
```

```python
import functools

import jax
import jax.numpy as jnp
from jax import lax
from jax.experimental import pallas as pl
from jax.experimental.pallas import tpu as pltpu
from jax.sharding import PartitionSpec as P

NT = 3072
EPS = 1e-05
LANES = 128
ROWS = 16
MESH = pl.DeviceIdType.MESH
F32 = jnp.float32
BF16 = jnp.bfloat16


def iota(shape, axis):
    return lax.broadcasted_iota(jnp.int32, shape, axis)


def kernel(
    n_t, n_s, sg_hbm, off_hbm, mov_hbm, wave_hbm, sig_hbm, out_ref,
    sg_ref, off_ref, mov_ref, wave_ref, pick, sig, asked, wanted, reply, landed, rows, toep, band, winv, wrev, stacks, parts,
    load_sem, ask_send, ask_recv, row_send, row_recv, part_send, part_recv,
):
    me_t = lax.axis_index("tmpl")
    me_s = lax.axis_index("stn")
    touch, n_k = sg_ref.shape
    n_slot = off_ref.shape[2]
    length = wave_ref.shape[3]
    chans, span = sig.shape
    slots = n_k * n_slot
    span_blocks = span // LANES
    all_blocks = span_blocks * n_t
    n_circ = -(-length // LANES)
    n_band = n_circ + 1
    out_blocks = NT // LANES
    chunks = slots // ROWS
    ahead = chunks // 2
    per_chunk = ROWS // n_slot
    own = n_k // n_s

    barrier = pltpu.get_barrier_semaphore()
    for d in range(1, n_t):
        pl.semaphore_signal(
            barrier, inc=1, device_id={"tmpl": lax.rem(me_t + d, n_t)}, device_id_type=MESH
        )
    for d in range(1, n_s):
        pl.semaphore_signal(
            barrier, inc=1, device_id={"stn": lax.rem(me_s + d, n_s)}, device_id_type=MESH
        )

    operands = (
        (sg_hbm, sg_ref), (off_hbm, off_ref), (sig_hbm, sig), (wave_hbm, wave_ref), (mov_hbm, mov_ref)
    )
    loads = [
        pltpu.make_async_copy(a, b, load_sem.at[i]) for i, (a, b) in enumerate(operands)
    ]
    for load in loads:
        load.start()

    gap = iota((n_band * LANES, LANES), 0) - iota((n_band * LANES, LANES), 1)
    band[...] = jnp.logical_and(gap >= 0, gap < length).astype(F32).astype(BF16)
    turn = jnp.bitwise_and(iota((LANES, LANES), 0) + iota((LANES, LANES), 1), LANES - 1)
    flip = (turn == 0).astype(F32).astype(BF16)

    loads[0].wait()
    loads[1].wait()

    lane = iota((n_slot, LANES), 1)
    sub = iota((n_slot, LANES), 0)
    tile = jnp.zeros((n_slot, LANES), jnp.int32)
    for k in range(n_k):
        at = jnp.int32(0)
        for g in range(1, touch):
            at = jnp.where(sg_ref[g, k] == me_s, g, at)
        pick[k] = at
        column = jnp.zeros((n_slot, LANES), jnp.int32)
        for s in range(n_slot):
            column = jnp.where(sub == s, off_ref[k, at, s], column)
        tile = jnp.where(lane == k, column, tile)
    asked[...] = tile

    pl.semaphore_wait(barrier, n_t - 1 + n_s - 1)

    def ask(d):
        return pltpu.make_async_remote_copy(
            src_ref=asked,
            dst_ref=wanted.at[d - 1],
            send_sem=ask_send.at[d - 1],
            recv_sem=ask_recv.at[d - 1],
            device_id={"tmpl": lax.rem(me_t + d, n_t)},
            device_id_type=MESH,
        )

    def send_rows(d, i):
        part = pl.ds(pl.multiple_of(i * ROWS, ROWS), ROWS)
        return pltpu.make_async_remote_copy(
            src_ref=reply.at[d - 1, part],
            dst_ref=landed.at[d - 1, part],
            send_sem=row_send.at[d - 1, i],
            recv_sem=row_recv.at[d - 1, i],
            device_id={"tmpl": lax.rem(me_t + n_t - d, n_t)},
            device_id_type=MESH,
        )

    for d in range(1, n_t):
        ask(d).start()

    piece = min(span, 512)

    def one_hot(tile):
        number = iota((n_slot, chans), 1)
        picked = [
            (number == jnp.broadcast_to(tile[:, k : k + 1], (n_slot, chans))).astype(F32)
            for k in range(n_k)
        ]
        return jnp.concatenate(picked, axis=0).astype(BF16)

    def order(i):
        return lax.rem(me_s * own // per_chunk + 1 + i, chunks)

    def place(tile, source, first):
        count = tile.shape[0]
        for j in range(tile.shape[1] // LANES):
            start = first * all_blocks + source * span_blocks + j
            rows[pl.ds(start, count, stride=all_blocks), :] = tile[:, j * LANES : (j + 1) * LANES]

    loads[3].wait()
    waves = []
    for k in range(n_k):
        live = sg_ref[0, k] == me_s
        for g in range(1, touch):
            live = jnp.logical_or(live, sg_ref[g, k] == me_s)
        wave = wave_ref[k, pick[k]].astype(F32)
        waves.append(jnp.where(live, wave, 0.0))
    waves = jnp.concatenate(waves, axis=0)
    power = jnp.sum(waves * waves, axis=1, keepdims=True) / length
    scale = lax.rsqrt(power + EPS) / length
    winv[...] = jnp.broadcast_to(scale, winv.shape)
    for j in range(n_circ):
        count = min(LANES, length - j * LANES)
        wrev[:, j * LANES : (j + 1) * LANES] = jnp.dot(
            waves[:, j * LANES : j * LANES + count].astype(BF16),
            flip[:count],
            preferred_element_type=F32,
        )

    loads[2].wait()
    for d in range(1, n_t):
        ask(d).wait_recv()
        theirs = one_hot(wanted[d - 1])
        for c in range(span // piece):
            cut = slice(c * piece, (c + 1) * piece)
            reply[d - 1, :, cut] = jnp.dot(
                theirs, sig[:, cut], preferred_element_type=F32
            ).astype(BF16)
        for i in range(ahead):
            send_rows(d, order(i)).start()

    mine = one_hot(tile)
    for c in range(span // piece):
        got = jnp.dot(mine, sig[:, c * piece : (c + 1) * piece], preferred_element_type=F32)
        for j in range(piece // LANES):
            start = me_t * span_blocks + c * (piece // LANES) + j
            rows[pl.ds(start, slots, stride=all_blocks), :] = got[:, j * LANES : (j + 1) * LANES]

    lower = (iota((LANES, LANES), 0) >= iota((LANES, LANES), 1)).astype(F32).astype(BF16) > 0

    def circle(line):
        first = pltpu.roll(jnp.broadcast_to(line, (ROWS, LANES)), 0, 1, stride=1, stride_axis=0)
        first = first.astype(BF16)
        return jnp.concatenate(
            [first] + [pltpu.roll(first, r, 1) for r in range(ROWS, LANES, ROWS)], axis=0
        )

    def build(k, carry):
        tile = wrev[pl.ds(pl.multiple_of(k * n_slot, n_slot), n_slot), :]
        zero = jnp.zeros((LANES, LANES), BF16)
        for s in range(n_slot):
            before = zero
            for j in range(n_band):
                here = zero
                if j < n_circ:
                    here = circle(tile[s : s + 1, j * LANES : (j + 1) * LANES])
                toep[k * n_slot + s, j * LANES : (j + 1) * LANES, :] = jnp.where(
                    lower, here, before
                )
                before = here
        return carry

    lax.fori_loop(0, n_k, build, 0)

    for d in range(1, n_t):
        for i in range(ahead):
            send_rows(d, order(i)).wait_send()
        for i in range(ahead, chunks):
            send_rows(d, order(i)).start()

    def send_part(k):
        return pltpu.make_async_remote_copy(
            src_ref=stacks.at[k],
            dst_ref=parts.at[me_s, lax.rem(k, own)],
            send_sem=part_send.at[k],
            recv_sem=part_recv.at[me_s, lax.rem(k, own)],
            device_id={"stn": k // own},
            device_id_type=MESH,
        )

    spot = iota((out_blocks, LANES), 1)
    loads[4].wait()

    def template(k):
        at = pick[k]
        segs = []
        prods = []
        for s in range(n_slot):
            move = mov_ref[k, at, s]
            blocks = move // LANES
            rest = move - blocks * LANES
            turn = lax.rem(LANES - rest, LANES)
            base = (k * n_slot + s) * all_blocks + blocks
            turned = [
                pltpu.roll(rows[pl.ds(base + j, out_blocks), :], turn, 1) for j in range(n_band + 1)
            ]
            keep = spot < LANES - rest
            seg = jnp.concatenate(
                [jnp.where(keep, turned[j], turned[j + 1]) for j in range(n_band)], axis=1
            )
            segs.append(seg)
            prods.append(
                jnp.dot(seg.astype(BF16), toep[k * n_slot + s], preferred_element_type=F32)
            )
        seg = jnp.concatenate(segs, axis=0)
        square = seg * seg
        high = square.astype(BF16)
        low = (square - high.astype(F32)).astype(BF16)
        bands = band[...]
        energy = jnp.dot(high, bands, preferred_element_type=F32)
        energy = energy + jnp.dot(low, bands, preferred_element_type=F32)
        inverse = lax.rsqrt(energy / length + EPS)
        scales = winv[pl.ds(pl.multiple_of(k * n_slot, n_slot), n_slot), :]
        total = jnp.zeros((out_blocks, LANES), F32)
        for s in range(n_slot):
            part = inverse[s * out_blocks : (s + 1) * out_blocks]
            total = total + prods[s] * (part * scales[s : s + 1, :])
        return total

    def chunk(step, carry):
        i = order(step)
        for d in range(1, n_t):
            send_rows(d, i).wait_recv()
            tile = landed[d - 1, pl.ds(pl.multiple_of(i * ROWS, ROWS), ROWS), :].astype(F32)
            place(tile, lax.rem(me_t + d, n_t), i * ROWS)
        names = [
            i * per_chunk + lax.rem(me_s * own + 1 + q, per_chunk) for q in range(per_chunk)
        ]
        totals = [template(k) for k in names]
        for k, total in zip(names, totals):
            stacks[k] = total
        for k in names:

            @pl.when(k // own != me_s)
            def _(k=k):
                send_part(k).start()

        return carry

    lax.fori_loop(0, chunks, chunk, 0)

    for d in range(1, n_t):
        ask(d).wait_send()
        for i in range(ahead, chunks):
            send_rows(d, order(i)).wait_send()

    for r in range(own):
        out_ref[r] = stacks[me_s * own + r]
    for d in range(1, n_s):
        other = lax.rem(me_s + d, n_s)
        for r in range(own):
            pltpu.make_async_remote_copy(
                src_ref=stacks.at[0],
                dst_ref=parts.at[other, r],
                send_sem=part_send.at[0],
                recv_sem=part_recv.at[other, r],
                device_id={"stn": other},
                device_id_type=MESH,
            ).wait_recv()
            out_ref[r] = out_ref[r] + parts[other, r]
    for d in range(1, n_s):
        other = lax.rem(me_s + d, n_s)
        for r in range(own):
            send_part(other * own + r).wait_send()


def shards(signal, waveforms, station_groups, channel_offsets, moveouts):
    n_t = lax.axis_size("tmpl")
    n_s = lax.axis_size("stn")
    n_k, touch, n_slot, length = waveforms.shape
    chans, span = signal.shape
    slots = n_k * n_slot
    out_blocks = NT // LANES
    n_circ = -(-length // LANES)
    chunks = slots // ROWS
    own = n_k // n_s
    dma = pltpu.SemaphoreType.DMA
    stack = pl.pallas_call(
        functools.partial(kernel, n_t, n_s),
        out_shape=jax.ShapeDtypeStruct((own, out_blocks, LANES), F32),
        in_specs=[pl.BlockSpec(memory_space=pl.ANY)] * 5,
        out_specs=pl.BlockSpec(memory_space=pltpu.VMEM),
        scratch_shapes=[
            pltpu.SMEM((touch, n_k), jnp.int32),
            pltpu.SMEM((n_k, touch, n_slot), jnp.int32),
            pltpu.SMEM((n_k, touch, n_slot), jnp.int32),
            pltpu.VMEM((n_k, touch, n_slot, length), BF16),
            pltpu.SMEM((n_k,), jnp.int32),
            pltpu.VMEM((chans, span), BF16),
            pltpu.VMEM((n_slot, LANES), jnp.int32),
            pltpu.VMEM((n_t - 1, n_slot, LANES), jnp.int32),
            pltpu.VMEM((n_t - 1, slots, span), BF16),
            pltpu.VMEM((n_t - 1, slots, span), BF16),
            pltpu.VMEM((slots * n_t * span // LANES, LANES), F32),
            pltpu.VMEM((slots, (n_circ + 1) * LANES, LANES), BF16),
            pltpu.VMEM(((n_circ + 1) * LANES, LANES), BF16),
            pltpu.VMEM((slots, LANES), F32),
            pltpu.VMEM((slots, n_circ * LANES), F32),
            pltpu.VMEM((n_k, out_blocks, LANES), F32),
            pltpu.VMEM((n_s, own, out_blocks, LANES), F32),
            dma((5,)),
            dma((n_t - 1,)),
            dma((n_t - 1,)),
            dma((n_t - 1, chunks)),
            dma((n_t - 1, chunks)),
            dma((n_k,)),
            dma((n_s, own)),
        ],
        compiler_params=pltpu.CompilerParams(
            collective_id=0, has_side_effects=True, vmem_limit_bytes=55212 * 1024
        ),
    )(station_groups.T, channel_offsets, moveouts, waveforms, signal)
    return stack.reshape(own, NT)


def solution(mesh):
    in_specs = (
        P("stn", ("span", "tmpl")),
        P("tmpl", None, None, None),
        P("tmpl", None),
        P("tmpl", None, None),
        P("tmpl", None, None),
    )
    out_specs = P(("tmpl", "stn"), "span")
    return jax.shard_map(shards, mesh=mesh, in_specs=in_specs, out_specs=out_specs, check_vma=False)
```

```python
import functools

import jax
import jax.numpy as jnp
from jax import lax
from jax.experimental import pallas as pl
from jax.experimental.pallas import tpu as pltpu
from jax.sharding import PartitionSpec as P

NT = 3072
EPS = 1e-05
LANES = 128
ROWS = 16
MESH = pl.DeviceIdType.MESH
F32 = jnp.float32
BF16 = jnp.bfloat16


def iota(shape, axis):
    return lax.broadcasted_iota(jnp.int32, shape, axis)


def kernel(
    n_t, n_s, sg_hbm, off_hbm, mov_hbm, wave_hbm, sig_hbm, out_ref,
    sg_ref, off_ref, mov_ref, wave_ref, pick, sig, asked, wanted, reply, landed, rows, toep, band, winv, wrev, stacks, parts,
    load_sem, ask_send, ask_recv, row_send, row_recv, part_send, part_recv,
):
    me_t = lax.axis_index("tmpl")
    me_s = lax.axis_index("stn")
    touch, n_k = sg_ref.shape
    n_slot = off_ref.shape[2]
    length = wave_ref.shape[3]
    chans, span = sig.shape
    slots = n_k * n_slot
    span_blocks = span // LANES
    pitch = span_blocks * n_t + 1
    n_circ = -(-length // LANES)
    n_band = n_circ + 1
    out_blocks = NT // LANES
    chunks = slots // ROWS
    per_chunk = ROWS // n_slot
    own = n_k // n_s

    barrier = pltpu.get_barrier_semaphore()
    for d in range(1, n_t):
        pl.semaphore_signal(
            barrier, inc=1, device_id={"tmpl": lax.rem(me_t + d, n_t)}, device_id_type=MESH
        )
    for d in range(1, n_s):
        pl.semaphore_signal(
            barrier, inc=1, device_id={"stn": lax.rem(me_s + d, n_s)}, device_id_type=MESH
        )

    operands = (
        (sg_hbm, sg_ref), (off_hbm, off_ref), (sig_hbm, sig), (wave_hbm, wave_ref), (mov_hbm, mov_ref)
    )
    loads = [
        pltpu.make_async_copy(a, b, load_sem.at[i]) for i, (a, b) in enumerate(operands)
    ]
    for load in loads:
        load.start()

    gap = iota((n_band * LANES, LANES), 0) - iota((n_band * LANES, LANES), 1)
    band[...] = jnp.logical_and(gap >= 0, gap < length).astype(F32).astype(BF16)
    turn = jnp.bitwise_and(iota((LANES, LANES), 0) + iota((LANES, LANES), 1), LANES - 1)
    flip = (turn == 0).astype(F32).astype(BF16)

    loads[0].wait()
    loads[1].wait()

    lane = iota((n_slot, LANES), 1)
    sub = iota((n_slot, LANES), 0)
    tile = jnp.zeros((n_slot, LANES), jnp.int32)
    for k in range(n_k):
        at = jnp.int32(0)
        for g in range(1, touch):
            at = jnp.where(sg_ref[g, k] == me_s, g, at)
        pick[k] = at
        column = jnp.zeros((n_slot, LANES), jnp.int32)
        for s in range(n_slot):
            column = jnp.where(sub == s, off_ref[k, at, s], column)
        tile = jnp.where(lane == k, column, tile)
    asked[...] = tile

    pl.semaphore_wait(barrier, n_t - 1 + n_s - 1)

    def ask(d):
        return pltpu.make_async_remote_copy(
            src_ref=asked,
            dst_ref=wanted.at[d - 1],
            send_sem=ask_send.at[d - 1],
            recv_sem=ask_recv.at[d - 1],
            device_id={"tmpl": lax.rem(me_t + d, n_t)},
            device_id_type=MESH,
        )

    def send_rows(d, i):
        part = pl.ds(pl.multiple_of(i * ROWS, ROWS), ROWS)
        return pltpu.make_async_remote_copy(
            src_ref=reply.at[d - 1, part],
            dst_ref=landed.at[d - 1, part],
            send_sem=row_send.at[d - 1, i],
            recv_sem=row_recv.at[d - 1, i],
            device_id={"tmpl": lax.rem(me_t + n_t - d, n_t)},
            device_id_type=MESH,
        )

    for d in range(1, n_t):
        ask(d).start()

    piece = min(span, 512)

    def one_hot(tile):
        number = iota((n_slot, chans), 1)
        picked = [
            (number == jnp.broadcast_to(tile[:, k : k + 1], (n_slot, chans))).astype(F32)
            for k in range(n_k)
        ]
        return jnp.concatenate(picked, axis=0).astype(BF16)

    def order(i):
        return lax.rem(me_s * own // per_chunk + 1 + i, chunks)

    def place(tile, source, first):
        count = tile.shape[0]
        for j in range(tile.shape[1] // LANES):
            start = first * pitch + source * span_blocks + j
            rows[pl.ds(start, count, stride=pitch), :] = tile[:, j * LANES : (j + 1) * LANES]

    loads[2].wait()
    mine = one_hot(tile)
    for c in range(span // piece):
        got = jnp.dot(mine, sig[:, c * piece : (c + 1) * piece], preferred_element_type=F32)
        for j in range(piece // LANES):
            start = me_t * span_blocks + c * (piece // LANES) + j
            rows[pl.ds(start, slots, stride=pitch), :] = got[:, j * LANES : (j + 1) * LANES]

    loads[3].wait()
    waves = []
    for k in range(n_k):
        live = sg_ref[0, k] == me_s
        for g in range(1, touch):
            live = jnp.logical_or(live, sg_ref[g, k] == me_s)
        wave = wave_ref[k, pick[k]].astype(F32)
        waves.append(jnp.where(live, wave, 0.0))
    waves = jnp.concatenate(waves, axis=0)
    power = jnp.sum(waves * waves, axis=1, keepdims=True) / length
    scale = lax.rsqrt(power + EPS) / length
    winv[...] = jnp.broadcast_to(scale, winv.shape)
    for j in range(n_circ):
        count = min(LANES, length - j * LANES)
        wrev[:, j * LANES : (j + 1) * LANES] = jnp.dot(
            waves[:, j * LANES : j * LANES + count].astype(BF16),
            flip[:count],
            preferred_element_type=F32,
        )

    for d in range(1, n_t):
        ask(d).wait_recv()
        theirs = one_hot(wanted[d - 1])
        for c in range(span // piece):
            cut = slice(c * piece, (c + 1) * piece)
            reply[d - 1, :, cut] = jnp.dot(
                theirs, sig[:, cut], preferred_element_type=F32
            ).astype(BF16)
        for i in range(chunks):
            send_rows(d, order(i)).start()

    lower = (iota((LANES, LANES), 0) >= iota((LANES, LANES), 1)).astype(F32).astype(BF16) > 0

    def circle(line):
        first = pltpu.roll(jnp.broadcast_to(line, (ROWS, LANES)), 0, 1, stride=1, stride_axis=0)
        first = first.astype(BF16)
        return jnp.concatenate(
            [first] + [pltpu.roll(first, r, 1) for r in range(ROWS, LANES, ROWS)], axis=0
        )

    def build(k, carry):
        tile = wrev[pl.ds(pl.multiple_of(k * n_slot, n_slot), n_slot), :]
        zero = jnp.zeros((LANES, LANES), BF16)
        for s in range(n_slot):
            before = zero
            for j in range(n_band):
                here = zero
                if j < n_circ:
                    here = circle(tile[s : s + 1, j * LANES : (j + 1) * LANES])
                toep[k * n_slot + s, j * LANES : (j + 1) * LANES, :] = jnp.where(
                    lower, here, before
                )
                before = here
        return carry

    lax.fori_loop(0, n_k, build, 0)

    def send_part(k):
        return pltpu.make_async_remote_copy(
            src_ref=stacks.at[k],
            dst_ref=parts.at[me_s, lax.rem(k, own)],
            send_sem=part_send.at[k],
            recv_sem=part_recv.at[me_s, lax.rem(k, own)],
            device_id={"stn": k // own},
            device_id_type=MESH,
        )

    spot = iota((out_blocks, LANES), 1)
    loads[4].wait()

    def template(k):
        at = pick[k]
        segs = []
        prods = []
        for s in range(n_slot):
            move = mov_ref[k, at, s]
            blocks = move // LANES
            rest = move - blocks * LANES
            turn = lax.rem(LANES - rest, LANES)
            base = (k * n_slot + s) * pitch + blocks
            turned = [
                pltpu.roll(rows[pl.ds(base + j, out_blocks), :], turn, 1) for j in range(n_band + 1)
            ]
            keep = spot < LANES - rest
            seg = jnp.concatenate(
                [jnp.where(keep, turned[j], turned[j + 1]) for j in range(n_band)], axis=1
            )
            segs.append(seg)
            prods.append(
                jnp.dot(seg.astype(BF16), toep[k * n_slot + s], preferred_element_type=F32)
            )
        seg = jnp.concatenate(segs, axis=0)
        square = seg * seg
        high = square.astype(BF16)
        low = (square - high.astype(F32)).astype(BF16)
        bands = band[...]
        energy = jnp.dot(high, bands, preferred_element_type=F32)
        energy = energy + jnp.dot(low, bands, preferred_element_type=F32)
        inverse = lax.rsqrt(energy / length + EPS)
        scales = winv[pl.ds(pl.multiple_of(k * n_slot, n_slot), n_slot), :]
        total = jnp.zeros((out_blocks, LANES), F32)
        for s in range(n_slot):
            part = inverse[s * out_blocks : (s + 1) * out_blocks]
            total = total + prods[s] * (part * scales[s : s + 1, :])
        return total

    def chunk(step, carry):
        i = order(step)
        for d in range(1, n_t):
            send_rows(d, i).wait_recv()
            tile = landed[d - 1, pl.ds(pl.multiple_of(i * ROWS, ROWS), ROWS), :].astype(F32)
            place(tile, lax.rem(me_t + d, n_t), i * ROWS)
        names = [
            i * per_chunk + lax.rem(me_s * own + 1 + q, per_chunk) for q in range(per_chunk)
        ]
        totals = [template(k) for k in names]
        for k, total in zip(names, totals):
            stacks[k] = total
        for k in names:

            @pl.when(k // own != me_s)
            def _(k=k):
                send_part(k).start()

        return carry

    lax.fori_loop(0, chunks, chunk, 0)

    for d in range(1, n_t):
        ask(d).wait_send()
        for i in range(chunks):
            send_rows(d, i).wait_send()

    for r in range(own):
        out_ref[r] = stacks[me_s * own + r]
    for d in range(1, n_s):
        other = lax.rem(me_s + d, n_s)
        for r in range(own):
            pltpu.make_async_remote_copy(
                src_ref=stacks.at[0],
                dst_ref=parts.at[other, r],
                send_sem=part_send.at[0],
                recv_sem=part_recv.at[other, r],
                device_id={"stn": other},
                device_id_type=MESH,
            ).wait_recv()
            out_ref[r] = out_ref[r] + parts[other, r]
    for d in range(1, n_s):
        other = lax.rem(me_s + d, n_s)
        for r in range(own):
            send_part(other * own + r).wait_send()


def shards(signal, waveforms, station_groups, channel_offsets, moveouts):
    n_t = lax.axis_size("tmpl")
    n_s = lax.axis_size("stn")
    n_k, touch, n_slot, length = waveforms.shape
    chans, span = signal.shape
    slots = n_k * n_slot
    out_blocks = NT // LANES
    n_circ = -(-length // LANES)
    chunks = slots // ROWS
    own = n_k // n_s
    dma = pltpu.SemaphoreType.DMA
    stack = pl.pallas_call(
        functools.partial(kernel, n_t, n_s),
        out_shape=jax.ShapeDtypeStruct((own, out_blocks, LANES), F32),
        in_specs=[pl.BlockSpec(memory_space=pl.ANY)] * 5,
        out_specs=pl.BlockSpec(memory_space=pltpu.VMEM),
        scratch_shapes=[
            pltpu.SMEM((touch, n_k), jnp.int32),
            pltpu.SMEM((n_k, touch, n_slot), jnp.int32),
            pltpu.SMEM((n_k, touch, n_slot), jnp.int32),
            pltpu.VMEM((n_k, touch, n_slot, length), BF16),
            pltpu.SMEM((n_k,), jnp.int32),
            pltpu.VMEM((chans, span), BF16),
            pltpu.VMEM((n_slot, LANES), jnp.int32),
            pltpu.VMEM((n_t - 1, n_slot, LANES), jnp.int32),
            pltpu.VMEM((n_t - 1, slots, span), BF16),
            pltpu.VMEM((n_t - 1, slots, span), BF16),
            pltpu.VMEM((slots * (n_t * span // LANES + 1), LANES), F32),
            pltpu.VMEM((slots, (n_circ + 1) * LANES, LANES), BF16),
            pltpu.VMEM(((n_circ + 1) * LANES, LANES), BF16),
            pltpu.VMEM((slots, LANES), F32),
            pltpu.VMEM((slots, n_circ * LANES), F32),
            pltpu.VMEM((n_k, out_blocks, LANES), F32),
            pltpu.VMEM((n_s, own, out_blocks, LANES), F32),
            dma((5,)),
            dma((n_t - 1,)),
            dma((n_t - 1,)),
            dma((n_t - 1, chunks)),
            dma((n_t - 1, chunks)),
            dma((n_k,)),
            dma((n_s, own)),
        ],
        compiler_params=pltpu.CompilerParams(
            collective_id=0, has_side_effects=True, vmem_limit_bytes=63 * 1024 * 1024
        ),
    )(station_groups.T, channel_offsets, moveouts, waveforms, signal)
    return stack.reshape(own, NT)


def solution(mesh):
    in_specs = (
        P("stn", ("span", "tmpl")),
        P("tmpl", None, None, None),
        P("tmpl", None),
        P("tmpl", None, None),
        P("tmpl", None, None),
    )
    out_specs = P(("tmpl", "stn"), "span")
    return jax.shard_map(shards, mesh=mesh, in_specs=in_specs, out_specs=out_specs, check_vma=False)
```
